32 devices in a mesh: ty: 4 (over y, core), tx: 8 (over z, x).
Axes of the slice: x: 2, y: 2, z: 4, core: 2. Of those that a mesh axis runs over, the one named last changes fastest.
Arguments:
- covariates: bfloat16 [65536, 512], P(('ty', 'tx')), may hold values from -6 to 6
- w_in: bfloat16 [512, 2048], replicated, may hold values from -0.25 to 0.25
- b_in: float32 [2048], replicated, may hold values from -3 to 3
- w_out: bfloat16 [2048, 128], replicated, may hold values from -0.125 to 0.125
- b_out: float32 [128], replicated, may hold values from -2 to 2
- owner: int32 [65536, 1], P(('ty', 'tx')), may hold values from 0 to 31; in each aligned block of 2048 rows (0 to 2047, 2048 to 4095, ...) at most 128 rows name the same one
- land_cell: int32 [65536], P(('ty', 'tx')), may hold values from 0 to 2047
- row_taps: float32 [128, 9], replicated, may hold values from 0.2 to 1
- col_taps: float32 [128, 9], replicated, may hold values from 0.2 to 1
- rate: float32 [128], replicated, may hold values from 0.2 to 1.5
- capacity: float32 [128], replicated, may hold values from 0.5 to 4
- observed: int32 [64, 1024, 128], P('ty', 'tx'), may hold values from 0 to 2
- surveyed: int32 [64, 1024], P('ty', 'tx'), may hold values 0 or 1
Outputs:
- density: float32 [64, 1024, 128], P('ty', 'tx')
- grad_w_in: float32 [512, 2048], P(('ty', 'tx'))
- grad_w_out: float32 [2048, 128], P(('ty', 'tx'))
The draws below stay inside these ranges and needn't reach their ends.
Inputs may be any that keep to these rules, and one draw needn't show every extreme that they name: `owner`: among the land cells of one device, no tile owns more than 128, and some tile owns exactly 128.
All inputs are finite; a program needn't handle non-finite values. No bound on the sum of `surveyed` on one device may be relied on, other than what follows from the above.
Results may differ from the reference program's by a relative error of at most 0.0017.
Values may be sent and summed in bfloat16 or wider, within the bound.
A program may use at most 128 MiB of HBM per device.

```python
import math
import jax
import jax.numpy as jnp
import numpy as np
from jax import lax

COV = 512
HID = 2048
S = 128
STEPS = 4
ROWS_DEV = 2048
TH = 16
TW = 128
CAP = 128
LAND = 65536
NR = 64
NC = 1024
N_TX = 8
DEVICES = 32


def set_ends(array, stream_key, least, high):
    dims = array.shape
    index_at = [jax.random.randint(jax.random.fold_in(stream_key, axis), (), 0, dims[axis]) for axis in range(len(dims))]
    array = array.at[tuple(index_at)].set(least)
    longest = dims.index(max(dims))
    index_at[longest] = (index_at[longest] + 1) % dims[longest]
    return array.at[tuple(index_at)].set(high)


def spiked(drawn, own_key, source, target, parts, factor):
    def block_of(position):
        return (jnp.arange(drawn.shape[position]) // (drawn.shape[position] // parts)).reshape((-1,) + (1,) * (drawn.ndim - 1 - position))

    near = jax.random.permutation(own_key, parts)[block_of(target)]
    far = (block_of(target) + parts // 2) % parts
    return jnp.where((block_of(source) == near) | (block_of(source) == far), factor * drawn, drawn)


def levels(key, extent, cuts, smallest, top_value):
    factor_of, own = 1.0, jax.random.fold_in(key, 6)
    for position, parts in cuts:
        steps = jnp.exp(jax.random.uniform(jax.random.fold_in(own, position), (parts,), jnp.float32, smallest / len(cuts), top_value / len(cuts)))
        factor_of = factor_of * jnp.repeat(steps, extent[position] // parts).reshape([-1 if axis == position else 1 for axis in range(len(extent))])
    return factor_of


def deal_out(own_key, own, number, rows, number_of, top, bound, skew):
    sequence = jax.random.permutation(own_key, number_of)
    heavy_load, usual = load_shares(number_of, rows * top, bound, skew, True), load_shares(number_of, rows * top, bound, skew, False)
    places = jnp.arange(number_of)

    def named(tallies, rotation):
        used = int((tallies > 0).sum())
        fixed = max(1, used // 4)
        moved = fixed + (places - fixed + rotation * (used - fixed)) % max(1, number_of - fixed)
        return jnp.zeros((number_of,), jnp.int32).at[sequence[jnp.where(places < fixed, places, moved)]].set(jnp.asarray(tallies, jnp.int32))

    tallies = jnp.where(number % 4 == 0, named(heavy_load, number // 4), named(usual, number - number // 4 - 1))
    mixed = jax.random.permutation(jax.random.fold_in(own, 3), number_of)
    source_of, sink = mixed[0:number_of // 2 * 2:2], mixed[1:number_of // 2 * 2:2]
    room = jnp.minimum(tallies[source_of] - 1, bound - tallies[sink]) // 2
    room = jnp.where((source_of == sequence[0]) | (sink == sequence[0]) | (tallies[sink] == 0), 0, jnp.maximum(room, 0))
    moved = jax.random.randint(jax.random.fold_in(own, 4), (number_of // 2,), 0, 1 << 20) % (room + 1)
    tallies = tallies.at[source_of].add(-moved).at[sink].add(moved)
    members = jnp.searchsorted(jnp.cumsum(tallies), jnp.arange(rows * top), side="right").astype(jnp.int32)
    table = members.reshape(top, rows).T
    table = table[jax.random.permutation(jax.random.fold_in(own, 1), rows)]
    rotation = jax.random.randint(jax.random.fold_in(own, 2), (rows, 1), 0, top)
    return jnp.take_along_axis(table, (jnp.arange(top)[None, :] + rotation) % top, axis=1)


def load_shares(amount, total, bound, slope, full):
    portions = [(1 << 20) // math.isqrt(rank ** slope) + 1 for rank in range(1, amount + 1)]
    largest = bound if full else min(bound, max(-(-total // amount), total * portions[0] // sum(portions)))
    least = 1 if total - largest >= amount - 1 else 0
    given, surplus = [largest] + [least] * (amount - 1), total - largest - least * (amount - 1)
    while surplus > 0:
        candidates = [i for i in range(1, amount) if given[i] < largest] or [i for i in range(1, amount) if given[i] < bound]
        whole, left = sum([portions[i] for i in candidates]), surplus
        for i in candidates:
            addition = min(bound - given[i], max(1, left * portions[i] // whole), surplus)
            given[i] = given[i] + addition
            surplus = surplus - addition
    return np.array(given)


def bell_draw(stream_key, dims, scale, limit, pieces=(), dtype=jnp.bfloat16):
    factor_of = levels(stream_key, dims, pieces, -0.22, 0.18) if pieces else 1.0
    values = jax.random.normal(stream_key, dims, jnp.float32) * scale * factor_of
    return jnp.minimum(jnp.maximum(values, -limit), limit).astype(dtype)


def bell_draw_with(stream_key, dims, width, bound, pieces, heavy, held_as=jnp.bfloat16):
    array = width * jax.random.normal(stream_key, dims, jnp.float32)
    if pieces:
        array = array * levels(stream_key, dims, pieces, -0.22, 0.18)
    return jnp.clip(spiked(array, jax.random.fold_in(stream_key, 3), *heavy), -bound, bound).astype(held_as)


def setup_inputs(seed: int = 0) -> dict:
    key_list = jax.random.split(jax.random.key(seed), 14)
    covariates = bell_draw_with(key_list[0], (LAND, COV), 1.0, 6.0, ((0, 32),), (0, 1, 32, 2.75))
    w_in = bell_draw(key_list[1], (COV, HID), COV ** -0.5, 0.25)
    b_in = bell_draw(key_list[2], (HID,), 0.5, 3.0, (), jnp.float32)
    w_out = bell_draw(key_list[3], (HID, S), HID ** -0.5, 0.125)
    b_out = bell_draw(key_list[4], (S,), 0.5, 2.0, (), jnp.float32)
    owner_keys = jax.random.split(jax.random.fold_in(key_list[5], 1), LAND // ROWS_DEV)
    owner_turns = jax.random.permutation(jax.random.fold_in(key_list[5], 3), LAND // ROWS_DEV)
    owner = jax.vmap(lambda own, number: deal_out(jax.random.fold_in(key_list[5], 2), own, number, ROWS_DEV, DEVICES, 1, CAP, 2))(owner_keys, owner_turns).reshape((LAND, 1))
    land_cell = set_ends(jax.random.randint(key_list[6], (LAND,), 0, TH * TW), jax.random.fold_in(key_list[6], 1), 0, (TH * TW) - 1).astype(jnp.int32)
    row_taps = jnp.clip(jnp.exp(jax.random.uniform(key_list[7], (S, 9), jnp.float32, math.log(0.2), math.log(1.0))), 0.2, 1.0)
    col_taps = jnp.clip(jnp.exp(jax.random.uniform(key_list[8], (S, 9), jnp.float32, math.log(0.2), math.log(1.0))), 0.2, 1.0)
    rate = jnp.clip(jnp.exp(jax.random.uniform(key_list[9], (S,), jnp.float32, math.log(0.2), math.log(1.5))), 0.2, 1.5)
    capacity = jnp.clip(jnp.exp(jax.random.uniform(key_list[10], (S,), jnp.float32, math.log(0.5), math.log(4.0))), 0.5, 4.0)
    observed = set_ends(jax.random.randint(key_list[11], (NR, NC, S), 0, 3), jax.random.fold_in(key_list[11], 1), 0, 2).astype(jnp.int32)
    surveyed = set_ends((jax.random.randint(key_list[12], (NR, NC), 0, 2) < 1).astype(jnp.int32), jax.random.fold_in(key_list[12], 1), 0, 1)
    return {"covariates": covariates, "w_in": w_in, "b_in": b_in, "w_out": w_out, "b_out": b_out, "owner": owner, "land_cell": land_cell, "row_taps": row_taps, "col_taps": col_taps, "rate": rate, "capacity": capacity, "observed": observed, "surveyed": surveyed}


def normalize(taps):
    return taps / lax.optimization_barrier(jnp.sum(taps, axis=1, keepdims=True))

def disperse_valid(padded, taps_y, taps_x):
    height = padded.shape[0] - 8
    width_out = padded.shape[1] - 8
    partial_rows = taps_y[:, 0] * padded[0:height]
    for offset in range(1, 9):
        partial_rows = partial_rows + taps_y[:, offset] * padded[offset:offset + height]
    result = taps_x[:, 0] * partial_rows[:, 0:width_out]
    for offset in range(1, 9):
        result = result + taps_x[:, offset] * partial_rows[:, offset:offset + width_out]
    return result

def silu_slope(value):
    sigmoid_v = jax.nn.sigmoid(value)
    return sigmoid_v + value * sigmoid_v * (1.0 - sigmoid_v)

def reference(covariates, w_in, b_in, w_out, b_out, owner, land_cell, row_taps, col_taps, rate, capacity, observed, surveyed):
    blocks = covariates.reshape(-1, ROWS_DEV, COV)

    def forward_block(block_rows):
        preact = jnp.dot(block_rows, w_in, preferred_element_type=jnp.float32) + b_in
        hidden = jax.nn.silu(preact).astype(jnp.bfloat16)
        log_rate = jnp.dot(hidden, w_out, preferred_element_type=jnp.float32) + b_out
        return jnp.exp(log_rate)
    intensity = lax.map(forward_block, blocks)
    sent = intensity.astype(jnp.bfloat16).reshape(-1, S)
    owner_flat = owner[:, 0]
    raster_row = (owner_flat // N_TX * TH + land_cell // TW).astype(jnp.int32)
    raster_col = (owner_flat % N_TX * TW + land_cell % TW).astype(jnp.int32)
    field = 0.1 + jnp.zeros((NR, NC, S), jnp.float32).at[raster_row, raster_col].add(sent.astype(jnp.float32))
    taps_y = normalize(row_taps)
    taps_x = normalize(col_taps)
    stored = []
    for step in range(STEPS):
        padded = jnp.pad(field, ((4, 4), (4, 4), (0, 0)))
        mid_value = disperse_valid(padded, taps_y, taps_x)
        stored.append(mid_value)
        field = mid_value * (1.0 + rate) / (1.0 + rate * mid_value / capacity)
    density = field
    scale = 1.0 / math.sqrt(LAND)
    grad_field = surveyed[:, :, None].astype(jnp.float32) * (1.0 - observed.astype(jnp.float32) / density) * scale
    for step in range(STEPS - 1, -1, -1):
        mid_value = stored[step]
        denom = 1.0 + rate * mid_value / capacity
        grad_mid = grad_field * (1.0 + rate) / (denom * denom)
        padded = jnp.pad(grad_mid, ((4, 4), (4, 4), (0, 0)))
        grad_field = disperse_valid(padded, taps_y[:, ::-1], taps_x[:, ::-1])
    returned = grad_field[raster_row, raster_col].astype(jnp.bfloat16)

    def backward_block(carry, items):
        block_rows, block_back = items
        preact = jnp.dot(block_rows, w_in, preferred_element_type=jnp.float32) + b_in
        hidden = jax.nn.silu(preact).astype(jnp.bfloat16)
        log_rate = jnp.dot(hidden, w_out, preferred_element_type=jnp.float32) + b_out
        dlog = (block_back.astype(jnp.float32) * jnp.exp(log_rate)).astype(jnp.bfloat16)
        grad_out = carry[1] + lax.dot_general(hidden, dlog, (((0,), (0,)), ((), ())), preferred_element_type=jnp.float32)
        dhidden = lax.dot_general(dlog, w_out, (((1,), (1,)), ((), ())), preferred_element_type=jnp.float32)
        dpre = (dhidden * silu_slope(preact)).astype(jnp.bfloat16)
        grad_in = carry[0] + lax.dot_general(block_rows, dpre, (((0,), (0,)), ((), ())), preferred_element_type=jnp.float32)
        return ((grad_in, grad_out), None)
    initial = (jnp.zeros((COV, HID), jnp.float32), jnp.zeros((HID, S), jnp.float32))
    totals, unused = lax.scan(backward_block, initial, (blocks, returned.reshape(-1, ROWS_DEV, S)))
    return (density, totals[0], totals[1])
```

```python
import functools
import math

import jax
import jax.numpy as jnp
from jax import lax
from jax.experimental import pallas as pl
from jax.experimental.pallas import tpu as pltpu
from jax.sharding import PartitionSpec as P

STEPS = 4
MESH = pl.DeviceIdType.MESH
VMEM_LIMIT = 56 * 1024 * 1024


def bit_list(tiles_y, tiles_x):
    bits = []
    for axis, count in (("ty", tiles_y), ("tx", tiles_x)):
        weight = count // 2
        while weight >= 1:
            bits.append((axis, weight))
            weight //= 2
    return bits


def stream_orders(tiles_y, tiles_x):
    bits = bit_list(tiles_y, tiles_x)
    core = ("ty", 1)
    rows = [b for b in bits if b[0] == "ty" and b[1] > 1]
    near = [b for b in bits if b[0] == "tx" and b[1] < tiles_x // 4]
    far = [b for b in bits if b[0] == "tx" and b[1] >= tiles_x // 4][::-1]
    return (
        [core] + rows + near + far,
        [core] + near + far + rows,
        [core] + far + near + rows,
    )


def stream_shapes(bits, order, rows, cols):
    left = list(bits)
    held, got = [], []
    for bit in order:
        place = left.index(bit)
        before, after = 2**place, 2 ** (len(left) - place - 1)
        held.append((before, 2, after, rows, cols))
        got.append((before, after, rows, cols))
        left.remove(bit)
    return held, got


def sum_kernel(tiles_y, tiles_x, plan, *refs):
    streams = len(plan)
    stages = len(plan[0][0])
    gin, gout, out_in, out_out = refs[:4]
    rest = list(refs[4:])
    got = [[rest.pop(0) for _ in range(stages)] for _ in range(streams)]
    held = [[None] + [rest.pop(0) for _ in range(stages - 1)] for _ in range(streams)]
    send_sem, recv_sem = rest
    at = {"ty": lax.axis_index("ty"), "tx": lax.axis_index("tx")}

    def side(bit):
        return lax.rem(at[bit[0]] // bit[1], 2)

    def partner(bit):
        axis, weight = bit
        moved = at[axis] + weight * (1 - 2 * side(bit))
        return (moved, at["tx"]) if axis == "ty" else (at["ty"], moved)

    barrier = pltpu.get_barrier_semaphore()
    for bit in bit_list(tiles_y, tiles_x):
        pl.semaphore_signal(barrier, inc=1, device_id=partner(bit), device_id_type=MESH)
    pl.semaphore_wait(barrier, stages)

    def source(s, k, which):
        order, first, cols = plan[s][0], plan[s][1], plan[s][2]
        if k > 0:
            return held[s][k].at[:, which]
        if first is None:
            return gout.at[:, which]
        return gin.at[:, which, :, :, first : first + cols]

    def copy(s, k):
        bit = plan[s][0][k]
        return pltpu.make_async_remote_copy(
            src_ref=source(s, k, 1 - side(bit)),
            dst_ref=got[s][k],
            send_sem=send_sem.at[s, k],
            recv_sem=recv_sem.at[s, k],
            device_id=partner(bit),
            device_id_type=MESH,
        )

    for s in range(streams):
        copy(s, 0).start()
    for k in range(stages):
        for s in range(streams):
            copy(s, k).wait_recv()
            mine = source(s, k, side(plan[s][0][k]))
            before, after = got[s][k].shape[:2]
            if k + 1 < stages:
                nxt = held[s][k + 1]
                after_n = nxt.shape[2]

                def add(i, _, mine=mine, theirs=got[s][k], nxt=nxt, after=after, after_n=after_n):
                    a, b = i // after, lax.rem(i, after)
                    nxt[i // (2 * after_n), lax.rem(i // after_n, 2), lax.rem(i, after_n)] = (
                        mine[a, b] + theirs[a, b]
                    )
                    return 0

                lax.fori_loop(0, before * after, add, 0)
                copy(s, k + 1).start()
            else:
                total = mine[0, 0] + got[s][k][0, 0]
                first, cols = plan[s][1], plan[s][2]
                if first is None:
                    out_out[...] = total
                else:
                    out_in[:, first : first + cols] = total
    for k in range(stages):
        for s in range(streams):
            copy(s, k).wait_send()


def sum_grads(grad_in, grad_out, tiles_y, tiles_x):
    devices = tiles_y * tiles_x
    rows_in, cols_in = grad_in.shape[0] // devices, grad_in.shape[1]
    rows_out, cols_out = grad_out.shape[0] // devices, grad_out.shape[1]
    bits = bit_list(tiles_y, tiles_x)
    orders = stream_orders(tiles_y, tiles_x)
    tile = cols_in // 16
    plan = [
        (orders[0], 0, 7 * tile, rows_in),
        (orders[1], 7 * tile, 7 * tile, rows_in),
        (orders[2], 14 * tile, 2 * tile, rows_in),
        (orders[2], None, cols_out, rows_out),
    ]
    held_all, got_all = [], []
    for order, first, cols, rows in plan:
        held, got = stream_shapes(bits, order, rows, cols)
        held_all += [pltpu.VMEM(s, jnp.float32) for s in held[1:]]
        got_all += [pltpu.VMEM(s, jnp.float32) for s in got]
    core_before, core_after = tiles_y // 2, tiles_x
    stages = len(bits)
    return pl.pallas_call(
        functools.partial(sum_kernel, tiles_y, tiles_x, plan),
        out_shape=(
            jax.ShapeDtypeStruct((rows_in, cols_in), jnp.float32),
            jax.ShapeDtypeStruct((rows_out, cols_out), jnp.float32),
        ),
        in_specs=[pl.BlockSpec(memory_space=pltpu.VMEM)] * 2,
        out_specs=(pl.BlockSpec(memory_space=pltpu.VMEM),) * 2,
        scratch_shapes=got_all
        + held_all
        + [
            pltpu.SemaphoreType.DMA((len(plan), stages)),
            pltpu.SemaphoreType.DMA((len(plan), stages)),
        ],
        compiler_params=pltpu.CompilerParams(
            collective_id=1, has_side_effects=True, vmem_limit_bytes=VMEM_LIMIT
        ),
        name="sum_grads",
    )(
        grad_in.reshape(core_before, 2, core_after, rows_in, cols_in),
        grad_out.reshape(core_before, 2, core_after, rows_out, cols_out),
    )


DIRS = ((-1, 0), (1, 0), (0, -1), (0, 1), (-1, -1), (-1, 1), (1, -1), (1, 1))


def raster_kernel(
    tiles_y,
    tiles_x,
    start_ref,
    taps_y_ref,
    taps_x_ref,
    rate_ref,
    cap_ref,
    obs_ref,
    sur_ref,
    density_ref,
    g0_ref,
    field,
    part,
    mids,
    y_out,
    y_in,
    send_sem,
    recv_sem,
):
    height, width, species = start_ref.shape
    at_y, at_x = lax.axis_index("ty"), lax.axis_index("tx")
    blocks = width // 8

    def exists(d):
        dy, dx = DIRS[d]
        conds = []
        if dy == -1:
            conds.append(at_y > 0)
        if dy == 1:
            conds.append(at_y < tiles_y - 1)
        if dx == -1:
            conds.append(at_x > 0)
        if dx == 1:
            conds.append(at_x < tiles_x - 1)
        return conds[0] if len(conds) == 1 else jnp.logical_and(*conds)

    def device(d):
        return (at_y + DIRS[d][0], at_x + DIRS[d][1])

    zero_rows = jnp.zeros((4, width + 16, species), jnp.float32)
    zero_cols = jnp.zeros((height, 8, species), jnp.float32)
    for p in range(2):
        field[p, 0:4] = zero_rows
        field[p, height + 4 : height + 8] = zero_rows
        field[p, 4 : height + 4, 0:8] = zero_cols
        field[p, 4 : height + 4, width + 8 : width + 16] = zero_cols
        for s in range(2):
            y_in[p, s] = jnp.zeros((4, width, species), jnp.bfloat16)

    def load_row(i, _):
        field[0, i + 4, 8 : width + 8] = start_ref[i]
        return 0

    lax.fori_loop(0, height, load_row, 0)

    barrier = pltpu.get_barrier_semaphore()
    for d in range(8):

        @pl.when(exists(d))
        def _(d=d):
            pl.semaphore_signal(barrier, inc=1, device_id=device(d), device_id_type=MESH)

    count_y = jnp.where(at_y > 0, 2, 1) + jnp.where(at_y < tiles_y - 1, 1, 0)
    count_x = jnp.where(at_x > 0, 2, 1) + jnp.where(at_x < tiles_x - 1, 1, 0)
    pl.semaphore_wait(barrier, count_y * count_x - 1)

    rows_of = {-1: (4, 8), 0: (4, height + 4), 1: (height, height + 4)}
    cols_of = {-1: (8, 16), 0: (8, width + 8), 1: (width, width + 8)}
    rows_to = {-1: (height + 4, height + 8), 0: (4, height + 4), 1: (0, 4)}
    cols_to = {-1: (width + 8, width + 16), 0: (8, width + 8), 1: (0, 8)}

    def copy(t, d):
        dy, dx = DIRS[d]
        p = t % 2
        if dx == 0:
            src, dst = y_out.at[p, 0 if dy == -1 else 1], y_in.at[p, 1 if dy == -1 else 0]
        else:
            r0, r1 = rows_of[dy]
            c0, c1 = cols_of[dx]
            src = field.at[p, r0:r1, c0:c1]
            r0, r1 = rows_to[dy]
            c0, c1 = cols_to[dx]
            dst = field.at[p, r0:r1, c0:c1]
        return pltpu.make_async_remote_copy(
            src_ref=src,
            dst_ref=dst,
            send_sem=send_sem.at[t, d],
            recv_sem=recv_sem.at[t, d],
            device_id=device(d),
            device_id_type=MESH,
        )

    def start(t, dirs):
        for d in dirs:

            @pl.when(exists(d))
            def _(d=d):
                copy(t, d).start()

    def stage_rows(t):
        p = t % 2
        for s, r0 in ((0, 4), (1, height)):
            for r in range(4):
                y_out[p, s, r] = field[p, r0 + r, 8 : width + 8].astype(jnp.bfloat16)

    opposite = [DIRS.index((-dy, -dx)) for dy, dx in DIRS]

    def finish(t):
        p = t % 2
        for d in range(8):

            @pl.when(exists(d))
            def _(d=d):
                copy(t, opposite[d]).wait_recv()

        for s, r0 in ((0, 0), (1, height + 4)):
            for r in range(4):
                field[p, r0 + r, 8 : width + 8] = y_in[p, s, r].astype(jnp.float32)

    def sent(t):
        for d in range(8):

            @pl.when(exists(d))
            def _(d=d):
                copy(t, d).wait_send()

    rate = jnp.broadcast_to(rate_ref[...], (8, species))
    grow = 1.0 + rate
    slope = rate / jnp.broadcast_to(cap_ref[...], (8, species))

    stage_rows(0)
    start(0, range(8))

    for t in range(2 * STEPS):
        p = t % 2
        order = range(9) if t < STEPS else range(8, -1, -1)
        taps_y = [taps_y_ref[a] for a in order]
        taps_x = [taps_x_ref[a] for a in order]
        finish(t)

        def down(c, _, p=p, taps_y=taps_y):
            cols = pl.ds(pl.multiple_of(c * 8, 8), 8)
            rows = [field[p, i, cols, :] for i in range(height + 8)]
            for i in range(height):
                pairs = [taps_y[a] * rows[i + a] for a in range(9)]
                while len(pairs) > 1:
                    pairs = [sum(pairs[j : j + 2][1:], pairs[j]) for j in range(0, len(pairs), 2)]
                part[i, cols, :] = pairs[0]
            return 0

        lax.fori_loop(0, blocks + 2, down, 0)
        if t + 1 < 2 * STEPS and t >= 1:
            sent(t - 1)

        def across(i, t=t, p=p, taps_x=taps_x):
            if t == STEPS - 1:
                seen = jnp.broadcast_to(sur_ref[pl.ds(i, 1), :], (width, width)).T
            for c in range(blocks):
                cols = slice(8 * c, 8 * c + 8)
                pairs = [taps_x[b] * part[i, 8 * c + 4 + b : 8 * c + 12 + b, :] for b in range(9)]
                while len(pairs) > 1:
                    pairs = [sum(pairs[j : j + 2][1:], pairs[j]) for j in range(0, len(pairs), 2)]
                value = pairs[0]
                if t == 2 * STEPS - 1:
                    g0_ref[i, cols, :] = value
                    continue
                if t < STEPS:
                    inverse = 1.0 / (1.0 + slope * value)
                    if t < STEPS - 1:
                        mids[t, i, cols, :] = value
                    new = value * grow * inverse
                    if t == STEPS - 1:
                        density_ref[i, cols, :] = new
                        ratio = obs_ref[i, cols, :].astype(jnp.float32) / new
                        value = seen[cols, :] * (1.0 - ratio)
                        new = value * grow * inverse * inverse
                else:
                    mid = mids[2 * STEPS - 2 - t, i, cols, :]
                    inverse = 1.0 / (1.0 + slope * mid)
                    new = value * grow * inverse * inverse
                field[1 - p, i + 4, 8 + 8 * c : 16 + 8 * c, :] = new

        def border(k, _):
            across(jnp.where(k < 4, k, k + (height - 8)))
            return 0

        def middle(k, _):
            across(k + 4)
            return 0

        lax.fori_loop(0, 8, border, 0)
        if t + 1 < 2 * STEPS:
            stage_rows(t + 1)
            start(t + 1, (0, 1, 4, 5, 6, 7))
        lax.fori_loop(0, height - 8, middle, 0)
        if t + 1 < 2 * STEPS:
            start(t + 1, (2, 3))
    sent(2 * STEPS - 2)
    sent(2 * STEPS - 1)


def raster_steps(start, taps_y, taps_x, rate, capacity, observed, seen, tiles_y, tiles_x):
    height, width, species = start.shape

    def wide(taps):
        return jnp.broadcast_to(taps.T[:, None, :], (9, 8, species))

    vmem = pl.BlockSpec(memory_space=pltpu.VMEM)
    return pl.pallas_call(
        functools.partial(raster_kernel, tiles_y, tiles_x),
        out_shape=(jax.ShapeDtypeStruct(start.shape, jnp.float32),) * 2,
        in_specs=[vmem] * 7,
        out_specs=(vmem,) * 2,
        scratch_shapes=[
            pltpu.VMEM((2, height + 8, width + 16, species), jnp.float32),
            pltpu.VMEM((height, width + 16, species), jnp.float32),
            pltpu.VMEM((STEPS - 1, height, width, species), jnp.float32),
            pltpu.VMEM((2, 2, 4, width, species), jnp.bfloat16),
            pltpu.VMEM((2, 2, 4, width, species), jnp.bfloat16),
            pltpu.SemaphoreType.DMA((2 * STEPS, 8)),
            pltpu.SemaphoreType.DMA((2 * STEPS, 8)),
        ],
        compiler_params=pltpu.CompilerParams(
            collective_id=2, has_side_effects=True, vmem_limit_bytes=VMEM_LIMIT
        ),
        name="raster_steps",
    )(
        start,
        wide(taps_y),
        wide(taps_x),
        rate.reshape(1, species),
        capacity.reshape(1, species),
        observed,
        seen,
    )


def normalize(taps):
    return taps / jnp.sum(taps, axis=1, keepdims=True)


def silu_slope(value):
    sigmoid_v = jax.nn.sigmoid(value)
    return sigmoid_v + value * sigmoid_v * (1.0 - sigmoid_v)


def local(
    covariates,
    w_in,
    b_in,
    w_out,
    b_out,
    owner,
    land_cell,
    row_taps,
    col_taps,
    rate,
    capacity,
    observed,
    surveyed,
):
    row_count = covariates.shape[0]
    tiles_y = lax.axis_size("ty")
    tiles_x = lax.axis_size("tx")
    devices = tiles_y * tiles_x
    slot_count = 2 * row_count // devices
    height, tile_width, species = observed.shape
    cell_count = height * tile_width
    preact = jnp.dot(covariates, w_in, preferred_element_type=jnp.float32) + b_in
    hidden = jax.nn.silu(preact).astype(jnp.bfloat16)
    log_rate = jnp.dot(hidden, w_out, preferred_element_type=jnp.float32) + b_out
    intensity = jnp.exp(log_rate)
    sent = intensity.astype(jnp.bfloat16)
    owner_rows = owner[:, 0]
    onehot = (owner_rows[:, None] == jnp.arange(devices, dtype=jnp.int32)[None, :]).astype(
        jnp.int32
    )
    before = jnp.cumsum(onehot, axis=0) - onehot
    slot_idx = jnp.sum(before * onehot, axis=1)
    flat_slot = owner_rows * slot_count + slot_idx
    send_values = jnp.zeros((devices * slot_count, species), jnp.bfloat16).at[flat_slot].set(sent)
    send_cells = (
        jnp.full((devices * slot_count,), cell_count, jnp.int32).at[flat_slot].set(land_cell)
    )
    got_values, got_cells = (
        lax.all_to_all(
            send_values.reshape(devices, slot_count, species),
            ("ty", "tx"),
            split_axis=0,
            concat_axis=0,
            tiled=True,
        ),
        lax.all_to_all(
            send_cells.reshape(devices, slot_count),
            ("ty", "tx"),
            split_axis=0,
            concat_axis=0,
            tiled=True,
        ),
    )
    cell_list = got_cells.reshape(-1)
    start_field = (
        jnp.zeros((cell_count, species), jnp.float32)
        .at[cell_list]
        .add(got_values.reshape(-1, species).astype(jnp.float32), mode="drop")
    )
    field = 0.1 + start_field.reshape(height, tile_width, species)
    taps_y = normalize(row_taps)
    taps_x = normalize(col_taps)
    scale = 1.0 / math.sqrt(row_count * devices)
    seen = surveyed.astype(jnp.float32) * scale
    field, grad_field = raster_steps(
        field, taps_y, taps_x, rate, capacity, observed, seen, tiles_y, tiles_x
    )
    back_values = jnp.take(
        grad_field.reshape(cell_count, species), cell_list, axis=0, mode="fill", fill_value=0.0
    ).astype(jnp.bfloat16)
    home_values = lax.all_to_all(
        back_values.reshape(devices, slot_count, species),
        ("ty", "tx"),
        split_axis=0,
        concat_axis=0,
        tiled=True,
    )
    returned = home_values.reshape(devices * slot_count, species)[flat_slot]
    dlog = (returned.astype(jnp.float32) * intensity).astype(jnp.bfloat16)
    dhidden = lax.dot_general(
        dlog, w_out, (((1,), (1,)), ((), ())), preferred_element_type=jnp.float32
    )
    dpre = (dhidden * silu_slope(preact)).astype(jnp.bfloat16)
    grad_w_in, grad_w_out = sum_grads(
        lax.dot_general(
            covariates, dpre, (((0,), (0,)), ((), ())), preferred_element_type=jnp.float32
        ),
        lax.dot_general(
            hidden, dlog, (((0,), (0,)), ((), ())), preferred_element_type=jnp.float32
        ),
        tiles_y,
        tiles_x,
    )
    return (field, grad_w_in, grad_w_out)


def solution(mesh):
    in_specs = (
        P(("ty", "tx"), None),
        P(),
        P(),
        P(),
        P(),
        P(("ty", "tx"), None),
        P(("ty", "tx")),
        P(),
        P(),
        P(),
        P(),
        P("ty", "tx", None),
        P("ty", "tx"),
    )
    out_specs = (P("ty", "tx", None), P(("ty", "tx"), None), P(("ty", "tx"), None))
    return jax.shard_map(local, mesh=mesh, in_specs=in_specs, out_specs=out_specs, check_vma=False)
```

```python
import functools
import math

import jax
import jax.numpy as jnp
from jax import lax
from jax.experimental import pallas as pl
from jax.experimental.pallas import tpu as pltpu
from jax.sharding import PartitionSpec as P

STEPS = 4
MESH = pl.DeviceIdType.MESH
VMEM_LIMIT = 56 * 1024 * 1024


def bit_list(tiles_y, tiles_x):
    bits = []
    for axis, count in (("ty", tiles_y), ("tx", tiles_x)):
        weight = count // 2
        while weight >= 1:
            bits.append((axis, weight))
            weight //= 2
    return bits


def stream_orders(tiles_y, tiles_x):
    bits = bit_list(tiles_y, tiles_x)
    core = ("ty", 1)
    rows = [b for b in bits if b[0] == "ty" and b[1] > 1]
    near = [b for b in bits if b[0] == "tx" and b[1] < tiles_x // 4]
    far = [b for b in bits if b[0] == "tx" and b[1] >= tiles_x // 4][::-1]
    return (
        [core] + rows + near + far,
        [core] + near + far + rows,
        [core] + far + near + rows,
    )


def stream_shapes(bits, order, rows, cols):
    left = list(bits)
    held, got = [], []
    for bit in order:
        place = left.index(bit)
        before, after = 2**place, 2 ** (len(left) - place - 1)
        held.append((before, 2, after, rows, cols))
        got.append((before, after, rows, cols))
        left.remove(bit)
    return held, got


def sum_kernel(tiles_y, tiles_x, plan, *refs):
    streams = len(plan)
    stages = len(plan[0][0])
    gin, gout, out_in, out_out = refs[:4]
    rest = list(refs[4:])
    got = [[rest.pop(0) for _ in range(stages)] for _ in range(streams)]
    held = [[None] + [rest.pop(0) for _ in range(stages - 1)] for _ in range(streams)]
    send_sem, recv_sem = rest
    at = {"ty": lax.axis_index("ty"), "tx": lax.axis_index("tx")}

    def side(bit):
        return lax.rem(at[bit[0]] // bit[1], 2)

    def partner(bit):
        axis, weight = bit
        moved = at[axis] + weight * (1 - 2 * side(bit))
        return (moved, at["tx"]) if axis == "ty" else (at["ty"], moved)

    barrier = pltpu.get_barrier_semaphore()
    for bit in bit_list(tiles_y, tiles_x):
        pl.semaphore_signal(barrier, inc=1, device_id=partner(bit), device_id_type=MESH)
    pl.semaphore_wait(barrier, stages)

    def source(s, k, which):
        order, first, cols = plan[s][0], plan[s][1], plan[s][2]
        if k > 0:
            return held[s][k].at[:, which]
        if first is None:
            return gout.at[:, which]
        return gin.at[:, which, :, :, first : first + cols]

    def copy(s, k):
        bit = plan[s][0][k]
        return pltpu.make_async_remote_copy(
            src_ref=source(s, k, 1 - side(bit)),
            dst_ref=got[s][k],
            send_sem=send_sem.at[s, k],
            recv_sem=recv_sem.at[s, k],
            device_id=partner(bit),
            device_id_type=MESH,
        )

    for s in range(streams):
        copy(s, 0).start()
    for k in range(stages):
        for s in range(streams):
            copy(s, k).wait_recv()
            mine = source(s, k, side(plan[s][0][k]))
            before, after = got[s][k].shape[:2]
            if k + 1 < stages:
                nxt = held[s][k + 1]
                after_n = nxt.shape[2]

                def add(i, _, mine=mine, theirs=got[s][k], nxt=nxt, after=after, after_n=after_n):
                    a, b = i // after, lax.rem(i, after)
                    nxt[i // (2 * after_n), lax.rem(i // after_n, 2), lax.rem(i, after_n)] = (
                        mine[a, b] + theirs[a, b]
                    )
                    return 0

                lax.fori_loop(0, before * after, add, 0)
                copy(s, k + 1).start()
            else:
                total = mine[0, 0] + got[s][k][0, 0]
                first, cols = plan[s][1], plan[s][2]
                if first is None:
                    out_out[...] = total
                else:
                    out_in[:, first : first + cols] = total
    for k in range(stages):
        for s in range(streams):
            copy(s, k).wait_send()


def sum_grads(grad_in, grad_out, tiles_y, tiles_x):
    devices = tiles_y * tiles_x
    rows_in, cols_in = grad_in.shape[0] // devices, grad_in.shape[1]
    rows_out, cols_out = grad_out.shape[0] // devices, grad_out.shape[1]
    bits = bit_list(tiles_y, tiles_x)
    orders = stream_orders(tiles_y, tiles_x)
    tile = cols_in // 16
    plan = [
        (orders[0], 0, 7 * tile, rows_in),
        (orders[1], 7 * tile, 7 * tile, rows_in),
        (orders[2], 14 * tile, 2 * tile, rows_in),
        (orders[2], None, cols_out, rows_out),
    ]
    held_all, got_all = [], []
    for order, first, cols, rows in plan:
        held, got = stream_shapes(bits, order, rows, cols)
        held_all += [pltpu.VMEM(s, jnp.float32) for s in held[1:]]
        got_all += [pltpu.VMEM(s, jnp.float32) for s in got]
    core_before, core_after = tiles_y // 2, tiles_x
    stages = len(bits)
    return pl.pallas_call(
        functools.partial(sum_kernel, tiles_y, tiles_x, plan),
        out_shape=(
            jax.ShapeDtypeStruct((rows_in, cols_in), jnp.float32),
            jax.ShapeDtypeStruct((rows_out, cols_out), jnp.float32),
        ),
        in_specs=[pl.BlockSpec(memory_space=pltpu.VMEM)] * 2,
        out_specs=(pl.BlockSpec(memory_space=pltpu.VMEM),) * 2,
        scratch_shapes=got_all
        + held_all
        + [
            pltpu.SemaphoreType.DMA((len(plan), stages)),
            pltpu.SemaphoreType.DMA((len(plan), stages)),
        ],
        compiler_params=pltpu.CompilerParams(
            collective_id=1, has_side_effects=True, vmem_limit_bytes=VMEM_LIMIT
        ),
        name="sum_grads",
    )(
        grad_in.reshape(core_before, 2, core_after, rows_in, cols_in),
        grad_out.reshape(core_before, 2, core_after, rows_out, cols_out),
    )


DIRS = ((-1, 0), (1, 0), (0, -1), (0, 1), (-1, -1), (-1, 1), (1, -1), (1, 1))


def raster_kernel(
    tiles_y,
    tiles_x,
    start_ref,
    taps_y_ref,
    taps_x_ref,
    rate_ref,
    cap_ref,
    obs_ref,
    sur_ref,
    density_ref,
    g0_ref,
    field,
    part,
    mids,
    y_out,
    y_in,
    send_sem,
    recv_sem,
):
    height, width, species = start_ref.shape
    at_y, at_x = lax.axis_index("ty"), lax.axis_index("tx")
    blocks = width // 8

    def exists(d):
        dy, dx = DIRS[d]
        conds = []
        if dy == -1:
            conds.append(at_y > 0)
        if dy == 1:
            conds.append(at_y < tiles_y - 1)
        if dx == -1:
            conds.append(at_x > 0)
        if dx == 1:
            conds.append(at_x < tiles_x - 1)
        return conds[0] if len(conds) == 1 else jnp.logical_and(*conds)

    def device(d):
        return (at_y + DIRS[d][0], at_x + DIRS[d][1])

    zero_rows = jnp.zeros((4, width + 16, species), jnp.float32)
    zero_cols = jnp.zeros((height, 8, species), jnp.float32)
    for p in range(2):
        field[p, 0:4] = zero_rows
        field[p, height + 4 : height + 8] = zero_rows
        field[p, 4 : height + 4, 0:8] = zero_cols
        field[p, 4 : height + 4, width + 8 : width + 16] = zero_cols
        for s in range(2):
            y_in[p, s] = jnp.zeros((4, width, species), jnp.bfloat16)

    def load_row(i, _):
        field[0, i + 4, 8 : width + 8] = start_ref[i]
        return 0

    lax.fori_loop(0, height, load_row, 0)

    barrier = pltpu.get_barrier_semaphore()
    for d in range(8):

        @pl.when(exists(d))
        def _(d=d):
            pl.semaphore_signal(barrier, inc=1, device_id=device(d), device_id_type=MESH)

    count_y = jnp.where(at_y > 0, 2, 1) + jnp.where(at_y < tiles_y - 1, 1, 0)
    count_x = jnp.where(at_x > 0, 2, 1) + jnp.where(at_x < tiles_x - 1, 1, 0)
    pl.semaphore_wait(barrier, count_y * count_x - 1)

    rows_of = {-1: (4, 8), 0: (4, height + 4), 1: (height, height + 4)}
    cols_of = {-1: (8, 16), 0: (8, width + 8), 1: (width, width + 8)}
    rows_to = {-1: (height + 4, height + 8), 0: (4, height + 4), 1: (0, 4)}
    cols_to = {-1: (width + 8, width + 16), 0: (8, width + 8), 1: (0, 8)}

    def copy(t, d):
        dy, dx = DIRS[d]
        p = t % 2
        if dx == 0:
            src, dst = y_out.at[p, 0 if dy == -1 else 1], y_in.at[p, 1 if dy == -1 else 0]
        else:
            r0, r1 = rows_of[dy]
            c0, c1 = cols_of[dx]
            src = field.at[p, r0:r1, c0:c1]
            r0, r1 = rows_to[dy]
            c0, c1 = cols_to[dx]
            dst = field.at[p, r0:r1, c0:c1]
        return pltpu.make_async_remote_copy(
            src_ref=src,
            dst_ref=dst,
            send_sem=send_sem.at[t, d],
            recv_sem=recv_sem.at[t, d],
            device_id=device(d),
            device_id_type=MESH,
        )

    def start(t, dirs):
        for d in dirs:

            @pl.when(exists(d))
            def _(d=d):
                copy(t, d).start()

    def stage_rows(t):
        p = t % 2
        for s, r0 in ((0, 4), (1, height)):
            for r in range(4):
                y_out[p, s, r] = field[p, r0 + r, 8 : width + 8].astype(jnp.bfloat16)

    opposite = [DIRS.index((-dy, -dx)) for dy, dx in DIRS]

    def finish(t):
        p = t % 2
        for d in range(8):

            @pl.when(exists(d))
            def _(d=d):
                copy(t, opposite[d]).wait_recv()

        for s, r0 in ((0, 0), (1, height + 4)):
            for r in range(4):
                field[p, r0 + r, 8 : width + 8] = y_in[p, s, r].astype(jnp.float32)

    def sent(t):
        for d in range(8):

            @pl.when(exists(d))
            def _(d=d):
                copy(t, d).wait_send()

    rate = jnp.broadcast_to(rate_ref[...], (8, species))
    grow = 1.0 + rate
    slope = rate / jnp.broadcast_to(cap_ref[...], (8, species))

    stage_rows(0)
    start(0, range(8))

    for t in range(2 * STEPS):
        p = t % 2
        order = range(9) if t < STEPS else range(8, -1, -1)
        taps_y = [taps_y_ref[a] for a in order]
        taps_x = [taps_x_ref[a] for a in order]
        finish(t)

        def down(c, _, p=p, taps_y=taps_y):
            cols = pl.ds(pl.multiple_of(c * 8, 8), 8)
            rows = [field[p, i, cols, :] for i in range(height + 8)]
            for i in range(height):
                pairs = [taps_y[a] * rows[i + a] for a in range(9)]
                while len(pairs) > 1:
                    pairs = [sum(pairs[j : j + 2][1:], pairs[j]) for j in range(0, len(pairs), 2)]
                part[i, cols, :] = pairs[0]
            return 0

        lax.fori_loop(0, blocks + 2, down, 0)
        if t + 1 < 2 * STEPS and t >= 1:
            sent(t - 1)

        def across(i, t=t, p=p, taps_x=taps_x):
            if t == STEPS - 1:
                seen = jnp.broadcast_to(sur_ref[pl.ds(i, 1), :], (width, width)).T
            for c in range(blocks):
                cols = slice(8 * c, 8 * c + 8)
                pairs = [taps_x[b] * part[i, 8 * c + 4 + b : 8 * c + 12 + b, :] for b in range(9)]
                while len(pairs) > 1:
                    pairs = [sum(pairs[j : j + 2][1:], pairs[j]) for j in range(0, len(pairs), 2)]
                value = pairs[0]
                if t == 2 * STEPS - 1:
                    g0_ref[i, cols, :] = value
                    continue
                if t < STEPS:
                    inverse = 1.0 / (1.0 + slope * value)
                    if t < STEPS - 1:
                        mids[t, i, cols, :] = value
                    new = value * grow * inverse
                    if t == STEPS - 1:
                        density_ref[i, cols, :] = new
                        ratio = obs_ref[i, cols, :].astype(jnp.float32) / new
                        value = seen[cols, :] * (1.0 - ratio)
                        new = value * grow * inverse * inverse
                else:
                    mid = mids[2 * STEPS - 2 - t, i, cols, :]
                    inverse = 1.0 / (1.0 + slope * mid)
                    new = value * grow * inverse * inverse
                field[1 - p, i + 4, 8 + 8 * c : 16 + 8 * c, :] = new

        def border(k, _):
            across(jnp.where(k < 4, k, k + (height - 8)))
            return 0

        def middle(k, _):
            across(k + 4)
            return 0

        lax.fori_loop(0, 8, border, 0)
        if t + 1 < 2 * STEPS:
            stage_rows(t + 1)
            start(t + 1, (0, 1, 4, 5, 6, 7))
        lax.fori_loop(0, height - 8, middle, 0)
        if t + 1 < 2 * STEPS:
            start(t + 1, (2, 3))
    sent(2 * STEPS - 2)
    sent(2 * STEPS - 1)


def raster_steps(start, taps_y, taps_x, rate, capacity, observed, seen, tiles_y, tiles_x):
    height, width, species = start.shape

    def wide(taps):
        return jnp.broadcast_to(taps.T[:, None, :], (9, 8, species))

    vmem = pl.BlockSpec(memory_space=pltpu.VMEM)
    return pl.pallas_call(
        functools.partial(raster_kernel, tiles_y, tiles_x),
        out_shape=(jax.ShapeDtypeStruct(start.shape, jnp.float32),) * 2,
        in_specs=[vmem] * 7,
        out_specs=(vmem,) * 2,
        scratch_shapes=[
            pltpu.VMEM((2, height + 8, width + 16, species), jnp.float32),
            pltpu.VMEM((height, width + 16, species), jnp.float32),
            pltpu.VMEM((STEPS - 1, height, width, species), jnp.float32),
            pltpu.VMEM((2, 2, 4, width, species), jnp.bfloat16),
            pltpu.VMEM((2, 2, 4, width, species), jnp.bfloat16),
            pltpu.SemaphoreType.DMA((2 * STEPS, 8)),
            pltpu.SemaphoreType.DMA((2 * STEPS, 8)),
        ],
        compiler_params=pltpu.CompilerParams(
            collective_id=2, has_side_effects=True, vmem_limit_bytes=VMEM_LIMIT
        ),
        name="raster_steps",
    )(
        start,
        wide(taps_y),
        wide(taps_x),
        rate.reshape(1, species),
        capacity.reshape(1, species),
        observed,
        seen,
    )


def local_call(body, shapes, args, scratch=(), name=None, **extra):
    vmem = pl.BlockSpec(memory_space=pltpu.VMEM)
    many = isinstance(shapes, tuple)
    return pl.pallas_call(
        body,
        out_shape=shapes,
        in_specs=[vmem] * len(args),
        out_specs=(vmem,) * len(shapes) if many else vmem,
        scratch_shapes=list(scratch),
        compiler_params=pltpu.CompilerParams(vmem_limit_bytes=VMEM_LIMIT),
        name=name,
        **extra,
    )(*args)


def sigmoid(value):
    return 0.5 + 0.5 * jnp.tanh(0.5 * value)


def forward_kernel(x_ref, w_in_ref, b_in_ref, w_out_ref, b_out_ref, intensity_ref):
    x = x_ref[...]
    hidden_units = w_in_ref.shape[1]
    log_rate = b_out_ref[...]
    for c in range(0, hidden_units, 512):
        pre = jnp.dot(x, w_in_ref[:, c : c + 512], preferred_element_type=jnp.float32)
        pre = pre + b_in_ref[:, c : c + 512]
        hidden = (pre * sigmoid(pre)).astype(jnp.bfloat16)
        log_rate = log_rate + jnp.dot(
            hidden, w_out_ref[c : c + 512, :], preferred_element_type=jnp.float32
        )
    intensity_ref[...] = jnp.exp(log_rate)


def forward(covariates, w_in, b_in, w_out, b_out):
    rows, cov = covariates.shape
    hid, species = w_out.shape
    block = 512
    return pl.pallas_call(
        forward_kernel,
        grid=(rows // block,),
        out_shape=jax.ShapeDtypeStruct((rows, species), jnp.float32),
        in_specs=[
            pl.BlockSpec((block, cov), lambda i: (i, 0)),
            pl.BlockSpec((cov, hid), lambda i: (0, 0)),
            pl.BlockSpec((1, hid), lambda i: (0, 0)),
            pl.BlockSpec((hid, species), lambda i: (0, 0)),
            pl.BlockSpec((1, species), lambda i: (0, 0)),
        ],
        out_specs=pl.BlockSpec((block, species), lambda i: (i, 0)),
        compiler_params=pltpu.CompilerParams(vmem_limit_bytes=VMEM_LIMIT),
        name="habitat_forward",
    )(covariates, w_in, b_in.reshape(1, hid), w_out, b_out.reshape(1, species))


def backward_kernel(x_ref, w_in_ref, b_in_ref, w_out_ref, dlog_ref, gin_ref, gout_ref, turned):
    step = pl.program_id(0)

    @pl.when(step == 0)
    def _():
        gin_ref[...] = jnp.zeros_like(gin_ref)
        turned[...] = jnp.zeros_like(turned)

    x = x_ref[...]
    dlog = dlog_ref[...]
    hidden_units = w_in_ref.shape[1]
    for c in range(0, hidden_units, 512):
        pre = jnp.dot(x, w_in_ref[:, c : c + 512], preferred_element_type=jnp.float32)
        pre = pre + b_in_ref[:, c : c + 512]
        sig = sigmoid(pre)
        act = pre * sig
        back = lax.dot_general(
            dlog,
            w_out_ref[c : c + 512, :],
            (((1,), (1,)), ((), ())),
            preferred_element_type=jnp.float32,
        )
        dpre = (back * (sig + act * (1.0 - sig))).astype(jnp.bfloat16)
        gin_ref[:, c : c + 512] += lax.dot_general(
            x, dpre, (((0,), (0,)), ((), ())), preferred_element_type=jnp.float32
        )
        turned[:, c : c + 512] += lax.dot_general(
            dlog,
            act.astype(jnp.bfloat16),
            (((0,), (0,)), ((), ())),
            preferred_element_type=jnp.float32,
        )

    @pl.when(step == pl.num_programs(0) - 1)
    def _():
        gout_ref[...] = turned[...].T


def backward(covariates, w_in, b_in, w_out, dlog):
    rows, cov = covariates.shape
    hid, species = w_out.shape
    block = 512
    return pl.pallas_call(
        backward_kernel,
        grid=(rows // block,),
        out_shape=(
            jax.ShapeDtypeStruct((cov, hid), jnp.float32),
            jax.ShapeDtypeStruct((hid, species), jnp.float32),
        ),
        in_specs=[
            pl.BlockSpec((block, cov), lambda i: (i, 0)),
            pl.BlockSpec((cov, hid), lambda i: (0, 0)),
            pl.BlockSpec((1, hid), lambda i: (0, 0)),
            pl.BlockSpec((hid, species), lambda i: (0, 0)),
            pl.BlockSpec((block, species), lambda i: (i, 0)),
        ],
        out_specs=(
            pl.BlockSpec((cov, hid), lambda i: (0, 0)),
            pl.BlockSpec((hid, species), lambda i: (0, 0)),
        ),
        scratch_shapes=[pltpu.VMEM((species, hid), jnp.float32)],
        compiler_params=pltpu.CompilerParams(vmem_limit_bytes=VMEM_LIMIT),
        name="habitat_backward",
    )(covariates, w_in, b_in.reshape(1, hid), w_out, dlog)


def iota(shape, dim):
    return lax.broadcasted_iota(jnp.int32, shape, dim)


def onehot(mask):
    return jnp.where(mask, 1.0, 0.0).astype(jnp.bfloat16)


def pack_kernel(slots, owner_ref, cell_ref, intensity_ref, send_ref, slot_ref, rows_ref, hot, wide):
    rows = owner_ref.shape[0]
    devices = send_ref.shape[0]
    chunk = 256
    below = onehot(iota((chunk, chunk), 0) > iota((chunk, chunk), 1))
    lane = iota((chunk, 128), 1)
    seen = jnp.zeros((1, 128), jnp.float32)
    for c in range(0, rows, chunk):
        owner = owner_ref[c : c + chunk, :]
        named = owner == lane
        hot_c = onehot(named)
        before = jnp.dot(below, hot_c, preferred_element_type=jnp.float32) + seen
        place = jnp.sum(jnp.where(named, before, 0.0), axis=1, keepdims=True)
        seen = seen + jnp.sum(jnp.where(named, 1.0, 0.0), axis=0, keepdims=True)
        flat = owner * slots + place.astype(jnp.int32)
        spread = jnp.broadcast_to(flat, (chunk, 128))
        slot_ref[c : c + chunk, :] = spread
        for h in range(0, chunk, 128):
            turned = spread[h : h + 128, :].astype(jnp.float32).T
            rows_ref[pl.ds((c + h) // 128, 1), :] = turned[0:1, :].astype(jnp.int32)
        cell = jnp.broadcast_to(cell_ref[c : c + chunk, :], (chunk, 128))
        high = cell // 128
        coded = jnp.where(lane == 0, high, jnp.where(lane == 1, cell - high * 128, 0))
        wide[c : c + chunk, 0:128] = intensity_ref[c : c + chunk, :].astype(jnp.bfloat16)
        wide[c : c + chunk, 128:256] = coded.astype(jnp.float32).astype(jnp.bfloat16)

    block = hot.shape[0]
    per_block = block // slots

    def step(m, _):
        row_id = iota((block, 128), 0) + m * block
        for j in range(rows // 128):
            hot[:, 128 * j : 128 * j + 128] = onehot(row_id == rows_ref[pl.ds(j, 1), :])
        packed = jnp.dot(hot[...], wide[...], preferred_element_type=jnp.float32)
        for q in range(per_block):
            part = packed[q * slots : (q + 1) * slots]
            target = m * per_block + q
            send_ref[target, 0:slots, :] = part[:, 0:128].astype(jnp.bfloat16)
            turned = part[:, 128:256].T[0:16]
            if slots < 128:
                turned = jnp.concatenate(
                    [turned, jnp.zeros((16, 128 - slots), jnp.float32)], axis=1
                )
            send_ref[target, slots : slots + 16, :] = turned.astype(jnp.bfloat16)
        return 0

    lax.fori_loop(0, devices // per_block, step, 0)


def pack(owner, land_cell, intensity, devices, slots):
    rows, species = intensity.shape
    block = min(1024, devices * slots)
    return local_call(
        functools.partial(pack_kernel, slots),
        (
            jax.ShapeDtypeStruct((devices, slots + 16, species), jnp.bfloat16),
            jax.ShapeDtypeStruct((rows, 128), jnp.int32),
        ),
        (owner, land_cell.reshape(rows, 1), intensity),
        scratch=(
            pltpu.VMEM((rows // 128, 128), jnp.int32),
            pltpu.VMEM((block, rows), jnp.bfloat16),
            pltpu.VMEM((rows, 256), jnp.bfloat16),
        ),
        name="pack",
    )


def cell_row(got_ref, d, slots):
    coded = got_ref[d, slots : slots + 16, :].astype(jnp.float32)
    return (coded[0:1, :] * 128.0 + coded[1:2, :]).astype(jnp.int32)


def place_kernel(slots, got_ref, start_ref, hot):
    devices = got_ref.shape[0]
    cells, block = hot.shape
    per_block = block // slots
    start_ref[...] = jnp.full(start_ref.shape, 0.1, jnp.float32)

    def step(m, _):
        for q in range(per_block):
            row = cell_row(got_ref, m * per_block + q, slots)
            mask = iota((cells, slots), 0) == row[:, 0:slots]
            hot[:, q * slots : (q + 1) * slots] = onehot(mask)
        values = got_ref[pl.ds(m * per_block, per_block), 0:slots, :].reshape(block, 128)
        start_ref[...] += jnp.dot(hot[...], values, preferred_element_type=jnp.float32)
        return 0

    lax.fori_loop(0, devices // per_block, step, 0)


def place(got, slots, cells):
    devices, _, species = got.shape
    block = min(1024, devices * slots)
    return local_call(
        functools.partial(place_kernel, slots),
        jax.ShapeDtypeStruct((cells, species), jnp.float32),
        (got,),
        scratch=(pltpu.VMEM((cells, block), jnp.bfloat16),),
        name="place",
    )


def collect_kernel(slots, got_ref, grad_ref, back_ref, hot, narrow):
    devices = got_ref.shape[0]
    block, cells = hot.shape
    per_block = block // slots
    narrow[...] = grad_ref[...].astype(jnp.bfloat16)

    def step(m, _):
        for q in range(per_block):
            row = cell_row(got_ref, m * per_block + q, slots)
            spread = jnp.broadcast_to(row.astype(jnp.float32), (128, 128)).T[0:slots]
            column = spread.astype(jnp.int32)
            for j in range(cells // 128):
                hot[q * slots : (q + 1) * slots, 128 * j : 128 * j + 128] = onehot(
                    column == iota((slots, 128), 1) + 128 * j
                )
        found = jnp.dot(hot[...], narrow[...], preferred_element_type=jnp.float32)
        back_ref[pl.ds(m * per_block, per_block)] = found.astype(jnp.bfloat16).reshape(
            per_block, slots, 128
        )
        return 0

    lax.fori_loop(0, devices // per_block, step, 0)


def collect(got, grad_field, slots):
    devices, _, species = got.shape
    cells = grad_field.shape[0]
    block = min(1024, devices * slots)
    return local_call(
        functools.partial(collect_kernel, slots),
        jax.ShapeDtypeStruct((devices, slots, species), jnp.bfloat16),
        (got, grad_field),
        scratch=(
            pltpu.VMEM((block, cells), jnp.bfloat16),
            pltpu.VMEM((cells, species), jnp.bfloat16),
        ),
        name="collect",
    )


def unpack_kernel(home_ref, slot_ref, intensity_ref, dlog_ref, hot):
    block, total = hot.shape
    rows = slot_ref.shape[0]

    def step(m, _):
        span = pl.ds(pl.multiple_of(m * block, block), block)
        for j in range(total // 128):
            hot[:, 128 * j : 128 * j + 128] = onehot(
                slot_ref[span, :] == iota((block, 128), 1) + 128 * j
            )
        returned = jnp.dot(hot[...], home_ref[...], preferred_element_type=jnp.float32)
        dlog_ref[span, :] = (returned * intensity_ref[span, :]).astype(jnp.bfloat16)
        return 0

    lax.fori_loop(0, rows // block, step, 0)


def unpack(home, slot, intensity):
    rows, species = intensity.shape
    return local_call(
        unpack_kernel,
        jax.ShapeDtypeStruct((rows, species), jnp.bfloat16),
        (home, slot, intensity),
        scratch=(pltpu.VMEM((512, home.shape[0]), jnp.bfloat16),),
        name="unpack",
    )


def normalize(taps):
    return taps / jnp.sum(taps, axis=1, keepdims=True)


def local(
    covariates,
    w_in,
    b_in,
    w_out,
    b_out,
    owner,
    land_cell,
    row_taps,
    col_taps,
    rate,
    capacity,
    observed,
    surveyed,
):
    row_count = covariates.shape[0]
    tiles_y = lax.axis_size("ty")
    tiles_x = lax.axis_size("tx")
    devices = tiles_y * tiles_x
    slot_count = 2 * row_count // devices
    height, tile_width, species = observed.shape
    cell_count = height * tile_width
    intensity = forward(covariates, w_in, b_in, w_out, b_out)
    send, slot = pack(owner, land_cell, intensity, devices, slot_count)
    got = lax.all_to_all(send, ("ty", "tx"), split_axis=0, concat_axis=0, tiled=True)
    start = place(got, slot_count, cell_count).reshape(height, tile_width, species)
    taps_y = normalize(row_taps)
    taps_x = normalize(col_taps)
    seen = surveyed.astype(jnp.float32) * (1.0 / math.sqrt(row_count * devices))
    field, grad_field = raster_steps(
        start, taps_y, taps_x, rate, capacity, observed, seen, tiles_y, tiles_x
    )
    back = collect(got, grad_field.reshape(cell_count, species), slot_count)
    home = lax.all_to_all(back, ("ty", "tx"), split_axis=0, concat_axis=0, tiled=True)
    dlog = unpack(home.reshape(devices * slot_count, species), slot, intensity)
    grad_w_in, grad_w_out = sum_grads(
        *backward(covariates, w_in, b_in, w_out, dlog), tiles_y, tiles_x
    )
    return (field, grad_w_in, grad_w_out)


def solution(mesh):
    in_specs = (
        P(("ty", "tx"), None),
        P(),
        P(),
        P(),
        P(),
        P(("ty", "tx"), None),
        P(("ty", "tx")),
        P(),
        P(),
        P(),
        P(),
        P("ty", "tx", None),
        P("ty", "tx"),
    )
    out_specs = (P("ty", "tx", None), P(("ty", "tx"), None), P(("ty", "tx"), None))
    return jax.shard_map(local, mesh=mesh, in_specs=in_specs, out_specs=out_specs, check_vma=False)
```

```python
import functools
import math

import jax
import jax.numpy as jnp
from jax import lax
from jax.experimental import pallas as pl
from jax.experimental.pallas import tpu as pltpu
from jax.sharding import PartitionSpec as P

STEPS = 4
MESH = pl.DeviceIdType.MESH
VMEM_LIMIT = 56 * 1024 * 1024


def bit_list(tiles_y, tiles_x):
    bits = []
    for axis, count in (("ty", tiles_y), ("tx", tiles_x)):
        weight = count // 2
        while weight >= 1:
            bits.append((axis, weight))
            weight //= 2
    return bits


def stream_orders(tiles_y, tiles_x):
    bits = bit_list(tiles_y, tiles_x)
    core = ("ty", 1)
    rows = [b for b in bits if b[0] == "ty" and b[1] > 1]
    near = [b for b in bits if b[0] == "tx" and b[1] < tiles_x // 4]
    far = [b for b in bits if b[0] == "tx" and b[1] >= tiles_x // 4][::-1]
    return (
        [core] + rows + near + far,
        [core] + near + far + rows,
        [core] + far + near + rows,
    )


def stream_shapes(bits, order, rows, cols):
    left = list(bits)
    held, got = [], []
    for bit in order:
        place = left.index(bit)
        before, after = 2**place, 2 ** (len(left) - place - 1)
        held.append((before, 2, after, rows, cols))
        got.append((before, after, rows, cols))
        left.remove(bit)
    return held, got


def sum_kernel(tiles_y, tiles_x, plan, *refs):
    streams = len(plan)
    stages = len(plan[0][0])
    gin, gout, out_in, out_out = refs[:4]
    rest = list(refs[4:])
    got = [[rest.pop(0) for _ in range(stages)] for _ in range(streams)]
    held = [[None] + [rest.pop(0) for _ in range(stages - 1)] for _ in range(streams)]
    send_sem, recv_sem = rest
    at = {"ty": lax.axis_index("ty"), "tx": lax.axis_index("tx")}

    def side(bit):
        return lax.rem(at[bit[0]] // bit[1], 2)

    def partner(bit):
        axis, weight = bit
        moved = at[axis] + weight * (1 - 2 * side(bit))
        return (moved, at["tx"]) if axis == "ty" else (at["ty"], moved)

    barrier = pltpu.get_barrier_semaphore()
    for bit in bit_list(tiles_y, tiles_x):
        pl.semaphore_signal(barrier, inc=1, device_id=partner(bit), device_id_type=MESH)
    pl.semaphore_wait(barrier, stages)

    def source(s, k, which):
        order, first, cols = plan[s][0], plan[s][1], plan[s][2]
        if k > 0:
            return held[s][k].at[:, which]
        if first is None:
            return gout.at[:, which]
        return gin.at[:, which, :, :, first : first + cols]

    def copy(s, k):
        bit = plan[s][0][k]
        return pltpu.make_async_remote_copy(
            src_ref=source(s, k, 1 - side(bit)),
            dst_ref=got[s][k],
            send_sem=send_sem.at[s, k],
            recv_sem=recv_sem.at[s, k],
            device_id=partner(bit),
            device_id_type=MESH,
        )

    for s in range(streams):
        copy(s, 0).start()
    for k in range(stages):
        for s in range(streams):
            copy(s, k).wait_recv()
            mine = source(s, k, side(plan[s][0][k]))
            before, after = got[s][k].shape[:2]
            if k + 1 < stages:
                nxt = held[s][k + 1]
                after_n = nxt.shape[2]

                def add(i, _, mine=mine, theirs=got[s][k], nxt=nxt, after=after, after_n=after_n):
                    a, b = i // after, lax.rem(i, after)
                    nxt[i // (2 * after_n), lax.rem(i // after_n, 2), lax.rem(i, after_n)] = (
                        mine[a, b] + theirs[a, b]
                    )
                    return 0

                lax.fori_loop(0, before * after, add, 0)
                copy(s, k + 1).start()
            else:
                total = mine[0, 0] + got[s][k][0, 0]
                first, cols = plan[s][1], plan[s][2]
                if first is None:
                    out_out[...] = total
                else:
                    out_in[:, first : first + cols] = total
    for k in range(stages):
        for s in range(streams):
            copy(s, k).wait_send()


def sum_grads(grad_in, grad_out, tiles_y, tiles_x):
    devices = tiles_y * tiles_x
    rows_in, cols_in = grad_in.shape[0] // devices, grad_in.shape[1]
    rows_out, cols_out = grad_out.shape[0] // devices, grad_out.shape[1]
    bits = bit_list(tiles_y, tiles_x)
    orders = stream_orders(tiles_y, tiles_x)
    tile = cols_in // 16
    plan = [
        (orders[0], 0, 7 * tile, rows_in),
        (orders[1], 7 * tile, 7 * tile, rows_in),
        (orders[2], 14 * tile, 2 * tile, rows_in),
        (orders[2], None, cols_out, rows_out),
    ]
    held_all, got_all = [], []
    for order, first, cols, rows in plan:
        held, got = stream_shapes(bits, order, rows, cols)
        held_all += [pltpu.VMEM(s, jnp.float32) for s in held[1:]]
        got_all += [pltpu.VMEM(s, jnp.float32) for s in got]
    core_before, core_after = tiles_y // 2, tiles_x
    stages = len(bits)
    return pl.pallas_call(
        functools.partial(sum_kernel, tiles_y, tiles_x, plan),
        out_shape=(
            jax.ShapeDtypeStruct((rows_in, cols_in), jnp.float32),
            jax.ShapeDtypeStruct((rows_out, cols_out), jnp.float32),
        ),
        in_specs=[pl.BlockSpec(memory_space=pltpu.VMEM)] * 2,
        out_specs=(pl.BlockSpec(memory_space=pltpu.VMEM),) * 2,
        scratch_shapes=got_all
        + held_all
        + [
            pltpu.SemaphoreType.DMA((len(plan), stages)),
            pltpu.SemaphoreType.DMA((len(plan), stages)),
        ],
        compiler_params=pltpu.CompilerParams(
            collective_id=1, has_side_effects=True, vmem_limit_bytes=VMEM_LIMIT
        ),
        name="sum_grads",
    )(
        grad_in.reshape(core_before, 2, core_after, rows_in, cols_in),
        grad_out.reshape(core_before, 2, core_after, rows_out, cols_out),
    )


DIRS = ((-1, 0), (1, 0), (0, -1), (0, 1), (-1, -1), (-1, 1), (1, -1), (1, 1))


def raster_kernel(
    tiles_y,
    tiles_x,
    start_ref,
    taps_y_ref,
    taps_x_ref,
    rate_ref,
    cap_ref,
    obs_ref,
    sur_ref,
    density_ref,
    g0_ref,
    field,
    part,
    mids,
    y_out,
    y_in,
    send_sem,
    recv_sem,
):
    height, width, species = start_ref.shape
    at_y, at_x = lax.axis_index("ty"), lax.axis_index("tx")
    blocks = width // 8

    def exists(d):
        dy, dx = DIRS[d]
        conds = []
        if dy == -1:
            conds.append(at_y > 0)
        if dy == 1:
            conds.append(at_y < tiles_y - 1)
        if dx == -1:
            conds.append(at_x > 0)
        if dx == 1:
            conds.append(at_x < tiles_x - 1)
        return conds[0] if len(conds) == 1 else jnp.logical_and(*conds)

    def device(d):
        return (at_y + DIRS[d][0], at_x + DIRS[d][1])

    zero_rows = jnp.zeros((4, width + 16, species), jnp.float32)
    zero_cols = jnp.zeros((height, 8, species), jnp.float32)
    for p in range(2):
        field[p, 0:4] = zero_rows
        field[p, height + 4 : height + 8] = zero_rows
        field[p, 4 : height + 4, 0:8] = zero_cols
        field[p, 4 : height + 4, width + 8 : width + 16] = zero_cols
        for s in range(2):
            y_in[p, s] = jnp.zeros((4, width, species), jnp.bfloat16)

    def load_row(i, _):
        field[0, i + 4, 8 : width + 8] = start_ref[i]
        return 0

    lax.fori_loop(0, height, load_row, 0)

    barrier = pltpu.get_barrier_semaphore()
    for d in range(8):

        @pl.when(exists(d))
        def _(d=d):
            pl.semaphore_signal(barrier, inc=1, device_id=device(d), device_id_type=MESH)

    count_y = jnp.where(at_y > 0, 2, 1) + jnp.where(at_y < tiles_y - 1, 1, 0)
    count_x = jnp.where(at_x > 0, 2, 1) + jnp.where(at_x < tiles_x - 1, 1, 0)
    pl.semaphore_wait(barrier, count_y * count_x - 1)

    rows_of = {-1: (4, 8), 0: (4, height + 4), 1: (height, height + 4)}
    cols_of = {-1: (8, 16), 0: (8, width + 8), 1: (width, width + 8)}
    rows_to = {-1: (height + 4, height + 8), 0: (4, height + 4), 1: (0, 4)}
    cols_to = {-1: (width + 8, width + 16), 0: (8, width + 8), 1: (0, 8)}

    def copy(t, d):
        dy, dx = DIRS[d]
        p = t % 2
        if dx == 0:
            src, dst = y_out.at[p, 0 if dy == -1 else 1], y_in.at[p, 1 if dy == -1 else 0]
        else:
            r0, r1 = rows_of[dy]
            c0, c1 = cols_of[dx]
            src = field.at[p, r0:r1, c0:c1]
            r0, r1 = rows_to[dy]
            c0, c1 = cols_to[dx]
            dst = field.at[p, r0:r1, c0:c1]
        return pltpu.make_async_remote_copy(
            src_ref=src,
            dst_ref=dst,
            send_sem=send_sem.at[t, d],
            recv_sem=recv_sem.at[t, d],
            device_id=device(d),
            device_id_type=MESH,
        )

    def start(t, dirs):
        for d in dirs:

            @pl.when(exists(d))
            def _(d=d):
                copy(t, d).start()

    def stage_rows(t):
        p = t % 2
        for s, r0 in ((0, 4), (1, height)):
            for r in range(4):
                y_out[p, s, r] = field[p, r0 + r, 8 : width + 8].astype(jnp.bfloat16)

    opposite = [DIRS.index((-dy, -dx)) for dy, dx in DIRS]

    def finish(t):
        p = t % 2
        for d in range(8):

            @pl.when(exists(d))
            def _(d=d):
                copy(t, opposite[d]).wait_recv()

        for s, r0 in ((0, 0), (1, height + 4)):
            for r in range(4):
                field[p, r0 + r, 8 : width + 8] = y_in[p, s, r].astype(jnp.float32)

    def sent(t):
        for d in range(8):

            @pl.when(exists(d))
            def _(d=d):
                copy(t, d).wait_send()

    rate = jnp.broadcast_to(rate_ref[...], (8, species))
    grow = 1.0 + rate
    slope = rate / jnp.broadcast_to(cap_ref[...], (8, species))

    stage_rows(0)
    start(0, range(8))

    for t in range(2 * STEPS):
        p = t % 2
        order = range(9) if t < STEPS else range(8, -1, -1)
        taps_y = [taps_y_ref[a] for a in order]
        taps_x = [taps_x_ref[a] for a in order]
        finish(t)

        def down(c, _, p=p, taps_y=taps_y):
            cols = pl.ds(pl.multiple_of(c * 8, 8), 8)
            rows = [field[p, i, cols, :] for i in range(height + 8)]
            for i in range(height):
                pairs = [taps_y[a] * rows[i + a] for a in range(9)]
                while len(pairs) > 1:
                    pairs = [sum(pairs[j : j + 2][1:], pairs[j]) for j in range(0, len(pairs), 2)]
                part[i, cols, :] = pairs[0]
            return 0

        lax.fori_loop(0, blocks + 2, down, 0)
        if t + 1 < 2 * STEPS and t >= 1:
            sent(t - 1)

        def across(i, t=t, p=p, taps_x=taps_x):
            if t == STEPS - 1:
                seen = jnp.broadcast_to(sur_ref[pl.ds(i, 1), :], (width, width)).T
            for c in range(blocks):
                cols = slice(8 * c, 8 * c + 8)
                pairs = [taps_x[b] * part[i, 8 * c + 4 + b : 8 * c + 12 + b, :] for b in range(9)]
                while len(pairs) > 1:
                    pairs = [sum(pairs[j : j + 2][1:], pairs[j]) for j in range(0, len(pairs), 2)]
                value = pairs[0]
                if t == 2 * STEPS - 1:
                    g0_ref[i, cols, :] = value
                    continue
                if t < STEPS:
                    inverse = 1.0 / (1.0 + slope * value)
                    if t < STEPS - 1:
                        mids[t, i, cols, :] = value
                    new = value * grow * inverse
                    if t == STEPS - 1:
                        density_ref[i, cols, :] = new
                        ratio = obs_ref[i, cols, :].astype(jnp.float32) / new
                        value = seen[cols, :] * (1.0 - ratio)
                        new = value * grow * inverse * inverse
                else:
                    mid = mids[2 * STEPS - 2 - t, i, cols, :]
                    inverse = 1.0 / (1.0 + slope * mid)
                    new = value * grow * inverse * inverse
                field[1 - p, i + 4, 8 + 8 * c : 16 + 8 * c, :] = new

        def border(k, _):
            across(jnp.where(k < 4, k, k + (height - 8)))
            return 0

        def middle(k, _):
            across(k + 4)
            return 0

        lax.fori_loop(0, 8, border, 0)
        if t + 1 < 2 * STEPS:
            stage_rows(t + 1)
            start(t + 1, (0, 1, 4, 5, 6, 7))
        lax.fori_loop(0, height - 8, middle, 0)
        if t + 1 < 2 * STEPS:
            start(t + 1, (2, 3))
    sent(2 * STEPS - 2)
    sent(2 * STEPS - 1)


def raster_steps(start, taps_y, taps_x, rate, capacity, observed, seen, tiles_y, tiles_x):
    height, width, species = start.shape

    def wide(taps):
        return jnp.broadcast_to(taps.T[:, None, :], (9, 8, species))

    vmem = pl.BlockSpec(memory_space=pltpu.VMEM)
    return pl.pallas_call(
        functools.partial(raster_kernel, tiles_y, tiles_x),
        out_shape=(jax.ShapeDtypeStruct(start.shape, jnp.float32),) * 2,
        in_specs=[vmem] * 7,
        out_specs=(vmem,) * 2,
        scratch_shapes=[
            pltpu.VMEM((2, height + 8, width + 16, species), jnp.float32),
            pltpu.VMEM((height, width + 16, species), jnp.float32),
            pltpu.VMEM((STEPS - 1, height, width, species), jnp.float32),
            pltpu.VMEM((2, 2, 4, width, species), jnp.bfloat16),
            pltpu.VMEM((2, 2, 4, width, species), jnp.bfloat16),
            pltpu.SemaphoreType.DMA((2 * STEPS, 8)),
            pltpu.SemaphoreType.DMA((2 * STEPS, 8)),
        ],
        compiler_params=pltpu.CompilerParams(
            collective_id=2, has_side_effects=True, vmem_limit_bytes=VMEM_LIMIT
        ),
        name="raster_steps",
    )(
        start,
        wide(taps_y),
        wide(taps_x),
        rate.reshape(1, species),
        capacity.reshape(1, species),
        observed,
        seen,
    )


def local_call(body, shapes, args, scratch=(), name=None, **extra):
    vmem = pl.BlockSpec(memory_space=pltpu.VMEM)
    many = isinstance(shapes, tuple)
    return pl.pallas_call(
        body,
        out_shape=shapes,
        in_specs=[vmem] * len(args),
        out_specs=(vmem,) * len(shapes) if many else vmem,
        scratch_shapes=list(scratch),
        compiler_params=pltpu.CompilerParams(vmem_limit_bytes=VMEM_LIMIT),
        name=name,
        **extra,
    )(*args)


def sigmoid(value):
    return 0.5 + 0.5 * jnp.tanh(0.5 * value)


def forward_kernel(x_ref, w_in_ref, b_in_ref, w_out_ref, b_out_ref, intensity_ref):
    x = x_ref[...]
    hidden_units = w_in_ref.shape[1]
    log_rate = b_out_ref[...]
    for c in range(0, hidden_units, 512):
        pre = jnp.dot(x, w_in_ref[:, c : c + 512], preferred_element_type=jnp.float32)
        pre = pre + b_in_ref[:, c : c + 512]
        hidden = (pre * sigmoid(pre)).astype(jnp.bfloat16)
        log_rate = log_rate + jnp.dot(
            hidden, w_out_ref[c : c + 512, :], preferred_element_type=jnp.float32
        )
    intensity_ref[...] = jnp.exp(log_rate)


def forward(covariates, w_in, b_in, w_out, b_out):
    rows, cov = covariates.shape
    hid, species = w_out.shape
    block = 512
    return pl.pallas_call(
        forward_kernel,
        grid=(rows // block,),
        out_shape=jax.ShapeDtypeStruct((rows, species), jnp.float32),
        in_specs=[
            pl.BlockSpec((block, cov), lambda i: (i, 0)),
            pl.BlockSpec((cov, hid), lambda i: (0, 0)),
            pl.BlockSpec((1, hid), lambda i: (0, 0)),
            pl.BlockSpec((hid, species), lambda i: (0, 0)),
            pl.BlockSpec((1, species), lambda i: (0, 0)),
        ],
        out_specs=pl.BlockSpec((block, species), lambda i: (i, 0)),
        compiler_params=pltpu.CompilerParams(vmem_limit_bytes=VMEM_LIMIT),
        name="habitat_forward",
    )(covariates, w_in, b_in.reshape(1, hid), w_out, b_out.reshape(1, species))


def prepare_kernel(x_ref, w_in_ref, b_in_ref, hidden_ref, slope_ref):
    x = x_ref[...]
    for c in range(0, w_in_ref.shape[1], 512):
        pre = jnp.dot(x, w_in_ref[:, c : c + 512], preferred_element_type=jnp.float32)
        pre = pre + b_in_ref[:, c : c + 512]
        sig = sigmoid(pre)
        act = pre * sig
        hidden_ref[:, c : c + 512] = act.astype(jnp.bfloat16)
        slope_ref[:, c : c + 512] = sig + act * (1.0 - sig)


def prepare(covariates, w_in, b_in):
    rows, cov = covariates.shape
    hid = w_in.shape[1]
    block = 512
    return pl.pallas_call(
        prepare_kernel,
        grid=(rows // block,),
        out_shape=(
            jax.ShapeDtypeStruct((rows, hid), jnp.bfloat16),
            jax.ShapeDtypeStruct((rows, hid), jnp.float32),
        ),
        in_specs=[
            pl.BlockSpec((block, cov), lambda i: (i, 0)),
            pl.BlockSpec((cov, hid), lambda i: (0, 0)),
            pl.BlockSpec((1, hid), lambda i: (0, 0)),
        ],
        out_specs=(pl.BlockSpec((block, hid), lambda i: (i, 0)),) * 2,
        compiler_params=pltpu.CompilerParams(vmem_limit_bytes=VMEM_LIMIT),
        cost_estimate=pl.CostEstimate(
            flops=2 * rows * cov * hid, bytes_accessed=8 * rows * hid, transcendentals=rows * hid
        ),
        name="habitat_prepare",
    )(covariates, w_in, b_in.reshape(1, hid))


def backward_kernel(x_ref, w_out_ref, dlog_ref, hidden_ref, slope_ref, gin_ref, gout_ref, turned):
    step = pl.program_id(0)

    @pl.when(step == 0)
    def _():
        gin_ref[...] = jnp.zeros_like(gin_ref)
        turned[...] = jnp.zeros_like(turned)

    x = x_ref[...]
    dlog = dlog_ref[...]
    for c in range(0, w_out_ref.shape[0], 512):
        back = lax.dot_general(
            dlog,
            w_out_ref[c : c + 512, :],
            (((1,), (1,)), ((), ())),
            preferred_element_type=jnp.float32,
        )
        dpre = (back * slope_ref[:, c : c + 512]).astype(jnp.bfloat16)
        gin_ref[:, c : c + 512] += lax.dot_general(
            x, dpre, (((0,), (0,)), ((), ())), preferred_element_type=jnp.float32
        )
        turned[:, c : c + 512] += lax.dot_general(
            dlog,
            hidden_ref[:, c : c + 512],
            (((0,), (0,)), ((), ())),
            preferred_element_type=jnp.float32,
        )

    @pl.when(step == pl.num_programs(0) - 1)
    def _():
        gout_ref[...] = turned[...].T


def backward(covariates, w_out, dlog, hidden, slope):
    rows, cov = covariates.shape
    hid, species = w_out.shape
    block = 512
    return pl.pallas_call(
        backward_kernel,
        grid=(rows // block,),
        out_shape=(
            jax.ShapeDtypeStruct((cov, hid), jnp.float32),
            jax.ShapeDtypeStruct((hid, species), jnp.float32),
        ),
        in_specs=[
            pl.BlockSpec((block, cov), lambda i: (i, 0)),
            pl.BlockSpec((hid, species), lambda i: (0, 0)),
            pl.BlockSpec((block, species), lambda i: (i, 0)),
            pl.BlockSpec((block, hid), lambda i: (i, 0)),
            pl.BlockSpec((block, hid), lambda i: (i, 0)),
        ],
        out_specs=(
            pl.BlockSpec((cov, hid), lambda i: (0, 0)),
            pl.BlockSpec((hid, species), lambda i: (0, 0)),
        ),
        scratch_shapes=[pltpu.VMEM((species, hid), jnp.float32)],
        compiler_params=pltpu.CompilerParams(vmem_limit_bytes=VMEM_LIMIT),
        name="habitat_backward",
    )(covariates, w_out, dlog, hidden, slope)


def iota(shape, dim):
    return lax.broadcasted_iota(jnp.int32, shape, dim)


def onehot(mask):
    return jnp.where(mask, 1.0, 0.0).astype(jnp.bfloat16)


def column(ref, first, count):
    tiles = []
    for r in range(first // 128, (first + count) // 128):
        row = ref[r : r + 1, :].astype(jnp.float32)
        tiles.append(jnp.broadcast_to(row, (128, 128)).T)
    return jnp.concatenate(tiles, axis=0).astype(jnp.int32)


def pack_kernel(slots, owner_ref, cell_ref, intensity_ref, send_ref, slot_ref, rows_ref, hot, wide):
    rows = intensity_ref.shape[0]
    devices = send_ref.shape[0]
    chunk = 256
    below = onehot(iota((chunk, chunk), 0) > iota((chunk, chunk), 1))
    lane = iota((chunk, 128), 1)
    seen = jnp.zeros((1, 128), jnp.float32)
    for c in range(0, rows, chunk):
        owner = column(owner_ref, c, chunk)
        named = owner == lane
        hot_c = onehot(named)
        before = jnp.dot(below, hot_c, preferred_element_type=jnp.float32) + seen
        place = jnp.sum(jnp.where(named, before, 0.0), axis=1, keepdims=True)
        seen = seen + jnp.sum(jnp.where(named, 1.0, 0.0), axis=0, keepdims=True)
        flat = owner * slots + place.astype(jnp.int32)
        spread = flat
        slot_ref[c : c + chunk, :] = spread
        for h in range(0, chunk, 128):
            turned = spread[h : h + 128, :].astype(jnp.float32).T
            rows_ref[pl.ds((c + h) // 128, 1), :] = turned[0:1, :].astype(jnp.int32)
        cell = column(cell_ref, c, chunk)
        high = cell // 128
        coded = jnp.where(lane == 0, high, jnp.where(lane == 1, cell - high * 128, 0))
        wide[c : c + chunk, 0:128] = intensity_ref[c : c + chunk, :].astype(jnp.bfloat16)
        wide[c : c + chunk, 128:256] = coded.astype(jnp.float32).astype(jnp.bfloat16)

    block = hot.shape[0]
    per_block = block // slots

    def step(m, _):
        row_id = iota((block, 128), 0) + m * block
        for j in range(rows // 128):
            hot[:, 128 * j : 128 * j + 128] = onehot(row_id == rows_ref[pl.ds(j, 1), :])
        packed = jnp.dot(hot[...], wide[...], preferred_element_type=jnp.float32)
        for q in range(per_block):
            part = packed[q * slots : (q + 1) * slots]
            target = m * per_block + q
            send_ref[target, 0:slots, :] = part[:, 0:128].astype(jnp.bfloat16)
            turned = part[:, 128:256].T[0:16]
            if slots < 128:
                turned = jnp.concatenate(
                    [turned, jnp.zeros((16, 128 - slots), jnp.float32)], axis=1
                )
            send_ref[target, slots : slots + 16, :] = turned.astype(jnp.bfloat16)
        return 0

    lax.fori_loop(0, devices // per_block, step, 0)


def pack(owner, land_cell, intensity, devices, slots):
    rows, species = intensity.shape
    block = min(1024, devices * slots)
    return local_call(
        functools.partial(pack_kernel, slots),
        (
            jax.ShapeDtypeStruct((devices, slots + 16, species), jnp.bfloat16),
            jax.ShapeDtypeStruct((rows, 128), jnp.int32),
        ),
        (owner.reshape(rows // 128, 128), land_cell.reshape(rows // 128, 128), intensity),
        scratch=(
            pltpu.VMEM((rows // 128, 128), jnp.int32),
            pltpu.VMEM((block, rows), jnp.bfloat16),
            pltpu.VMEM((rows, 256), jnp.bfloat16),
        ),
        name="pack",
    )


def cell_row(got_ref, d, slots):
    coded = got_ref[d, slots : slots + 16, :].astype(jnp.float32)
    return (coded[0:1, :] * 128.0 + coded[1:2, :]).astype(jnp.int32)


def place_kernel(slots, got_ref, start_ref, hot):
    devices = got_ref.shape[0]
    cells, block = hot.shape
    per_block = block // slots
    start_ref[...] = jnp.full(start_ref.shape, 0.1, jnp.float32)

    def step(m, _):
        for q in range(per_block):
            row = cell_row(got_ref, m * per_block + q, slots)
            mask = iota((cells, slots), 0) == row[:, 0:slots]
            hot[:, q * slots : (q + 1) * slots] = onehot(mask)
        values = got_ref[pl.ds(m * per_block, per_block), 0:slots, :].reshape(block, 128)
        start_ref[...] += jnp.dot(hot[...], values, preferred_element_type=jnp.float32)
        return 0

    lax.fori_loop(0, devices // per_block, step, 0)


def place(got, slots, cells):
    devices, _, species = got.shape
    block = min(1024, devices * slots)
    return local_call(
        functools.partial(place_kernel, slots),
        jax.ShapeDtypeStruct((cells, species), jnp.float32),
        (got,),
        scratch=(pltpu.VMEM((cells, block), jnp.bfloat16),),
        name="place",
    )


def collect_kernel(slots, got_ref, grad_ref, back_ref, hot, narrow):
    devices = got_ref.shape[0]
    block, cells = hot.shape
    per_block = block // slots
    narrow[...] = grad_ref[...].astype(jnp.bfloat16)

    def step(m, _):
        for q in range(per_block):
            row = cell_row(got_ref, m * per_block + q, slots)
            spread = jnp.broadcast_to(row.astype(jnp.float32), (128, 128)).T[0:slots]
            column = spread.astype(jnp.int32)
            for j in range(cells // 128):
                hot[q * slots : (q + 1) * slots, 128 * j : 128 * j + 128] = onehot(
                    column == iota((slots, 128), 1) + 128 * j
                )
        found = jnp.dot(hot[...], narrow[...], preferred_element_type=jnp.float32)
        back_ref[pl.ds(m * per_block, per_block)] = found.astype(jnp.bfloat16).reshape(
            per_block, slots, 128
        )
        return 0

    lax.fori_loop(0, devices // per_block, step, 0)


def collect(got, grad_field, slots):
    devices, _, species = got.shape
    cells = grad_field.shape[0]
    block = min(1024, devices * slots)
    return local_call(
        functools.partial(collect_kernel, slots),
        jax.ShapeDtypeStruct((devices, slots, species), jnp.bfloat16),
        (got, grad_field),
        scratch=(
            pltpu.VMEM((block, cells), jnp.bfloat16),
            pltpu.VMEM((cells, species), jnp.bfloat16),
        ),
        name="collect",
    )


def unpack_kernel(home_ref, slot_ref, intensity_ref, dlog_ref, hot):
    block, total = hot.shape
    rows = slot_ref.shape[0]

    def step(m, _):
        span = pl.ds(pl.multiple_of(m * block, block), block)
        for j in range(total // 128):
            hot[:, 128 * j : 128 * j + 128] = onehot(
                slot_ref[span, :] == iota((block, 128), 1) + 128 * j
            )
        returned = jnp.dot(hot[...], home_ref[...], preferred_element_type=jnp.float32)
        dlog_ref[span, :] = (returned * intensity_ref[span, :]).astype(jnp.bfloat16)
        return 0

    lax.fori_loop(0, rows // block, step, 0)


def unpack(home, slot, intensity):
    rows, species = intensity.shape
    return local_call(
        unpack_kernel,
        jax.ShapeDtypeStruct((rows, species), jnp.bfloat16),
        (home, slot, intensity),
        scratch=(pltpu.VMEM((512, home.shape[0]), jnp.bfloat16),),
        name="unpack",
    )


def normalize(taps):
    return taps / jnp.sum(taps, axis=1, keepdims=True)


def local(
    covariates,
    w_in,
    b_in,
    w_out,
    b_out,
    owner,
    land_cell,
    row_taps,
    col_taps,
    rate,
    capacity,
    observed,
    surveyed,
):
    row_count = covariates.shape[0]
    tiles_y = lax.axis_size("ty")
    tiles_x = lax.axis_size("tx")
    devices = tiles_y * tiles_x
    slot_count = 2 * row_count // devices
    height, tile_width, species = observed.shape
    cell_count = height * tile_width
    intensity = forward(covariates, w_in, b_in, w_out, b_out)
    send, slot = pack(owner, land_cell, intensity, devices, slot_count)
    bias, send = lax.optimization_barrier((b_in, send))
    got = lax.all_to_all(send, ("ty", "tx"), split_axis=0, concat_axis=0, tiled=True)
    hidden, slope = prepare(covariates, w_in, bias)
    got, hidden, slope = lax.optimization_barrier((got, hidden, slope))
    start = place(got, slot_count, cell_count).reshape(height, tile_width, species)
    taps_y = normalize(row_taps)
    taps_x = normalize(col_taps)
    seen = surveyed.astype(jnp.float32) * (1.0 / math.sqrt(row_count * devices))
    field, grad_field = raster_steps(
        start, taps_y, taps_x, rate, capacity, observed, seen, tiles_y, tiles_x
    )
    back = collect(got, grad_field.reshape(cell_count, species), slot_count)
    home = lax.all_to_all(back, ("ty", "tx"), split_axis=0, concat_axis=0, tiled=True)
    dlog = unpack(home.reshape(devices * slot_count, species), slot, intensity)
    grad_w_in, grad_w_out = sum_grads(
        *backward(covariates, w_out, dlog, hidden, slope), tiles_y, tiles_x
    )
    return (field, grad_w_in, grad_w_out)


def solution(mesh):
    in_specs = (
        P(("ty", "tx"), None),
        P(),
        P(),
        P(),
        P(),
        P(("ty", "tx"), None),
        P(("ty", "tx")),
        P(),
        P(),
        P(),
        P(),
        P("ty", "tx", None),
        P("ty", "tx"),
    )
    out_specs = (P("ty", "tx", None), P(("ty", "tx"), None), P(("ty", "tx"), None))
    return jax.shard_map(local, mesh=mesh, in_specs=in_specs, out_specs=out_specs, check_vma=False)
```
